32 devices in a mesh: groups: 2 (over y), blk: 4 (over z), rep: 4 (over x, core).
Axes of the slice: x: 2, y: 2, z: 4, core: 2. Of those that a mesh axis runs over, the one named last changes fastest.
Arguments:
- features: bfloat16 [4096, 512], P(('groups', 'blk', 'rep')), parts along dimension 0, may hold values from -6 to 6
- order_weights: bfloat16 [3, 512, 512], replicated, may hold values from -0.15625 to 0.15625
- laplacian_blocks: bfloat16 [8, 4, 4, 4, 128, 128], P(('groups', 'blk'), 'rep'), parts along dimension 0, may hold values from -0.15625 to 0.15625
- tile_place: int32 [8, 4, 4, 4], P(('groups', 'blk'), 'rep'), parts along dimension 0, may hold values from 0 to 3, as said below
- tile_count: int32 [8, 4, 4], P(('groups', 'blk'), 'rep'), parts along dimension 0, may hold values from 1 to 4
Outputs:
- mixed: bfloat16 [4096, 512], P(('groups', 'blk', 'rep')), parts along dimension 0
The draws below stay inside these ranges and needn't reach their ends.
There are 2 independent parts, one for each index of `groups`. The reference program is written for one: setup_inputs(seed, part) draws one part's arguments, and reference() takes and returns one part's arrays. A program takes and returns all parts, laid end to end along the dimension named above; an argument that names none is the same for every part. Nothing has to cross between parts.
Inputs may be any that keep to these rules, and one draw needn't show every extreme that they name: `tile_place`: within each strip, lane and source strip the 4 positions are distinct numbers below 4; only the first tile_count slots are live.
All inputs are finite; a program needn't handle non-finite values.
Results may differ from the reference program's by a relative error of at most 0.0055.
Values may be sent and summed in bfloat16 or wider, within the bound.
No kernel may reach another device: no remote copies, remote signals or barrier semaphores. Data moves between devices by JAX's collectives and lax.ppermute only.
A program may use at most 64 MiB of HBM per device.

```python
import jax
import jax.numpy as jnp
from jax import lax

F = 512
TILE = 128
RDEV = 128
STRIP = 512
NODES = 2048
ROWT = 4
COLT = 1
CAP = 4
N_BLK = 4
N_REP = 4


def draw_tile_place(key, part):
    key = jax.random.fold_in(key, 11)
    blk_count = NODES // STRIP
    rep_count = STRIP // RDEV
    spots = ROWT * COLT
    scores = jax.random.randint(key, (blk_count, rep_count, blk_count, spots), 0, 1 << 20) * spots + jnp.arange(spots)
    return jnp.argsort(scores, axis=-1)[..., :CAP].astype(jnp.int32)


def draw_tile_count(key, part):
    key = jax.random.fold_in(key, 12)
    blk_count = NODES // STRIP
    rep_count = STRIP // RDEV
    counts = jax.random.randint(key, (blk_count, rep_count, blk_count), max(1, CAP // 4), CAP + 1)
    diagonal = jnp.arange(blk_count)[:, None, None] == jnp.arange(blk_count)[None, None, :]
    return jnp.where(diagonal, CAP, counts).astype(jnp.int32)


def steps_of(stream_key, dims, shards, smallest, high):
    level, own = 1.0, jax.random.fold_in(stream_key, 6)
    for axis_at, parts in shards:
        heights = jnp.exp(jax.random.uniform(jax.random.fold_in(own, axis_at), (parts,), jnp.float32, smallest / len(shards), high / len(shards)))
        level = level * jnp.repeat(heights, dims[axis_at] // parts).reshape([-1 if axis == axis_at else 1 for axis in range(len(dims))])
    return level


def scatter_about(stream_key, extent, width, bound, split=(), kind=jnp.bfloat16):
    result = jax.random.normal(stream_key, extent, jnp.float32) * width
    if len(split) > 0:
        result = steps_of(stream_key, extent, split, -0.22, 0.18) * result
    return jnp.clip(result, min=-bound, max=bound).astype(kind)


def setup_inputs(seed: int = 0, part: int = 0) -> dict:
    key_of = jax.random.split(jax.random.key(seed), 6)
    own_keys = jax.random.split(jax.random.fold_in(key_of[5], part), 6)
    features = scatter_about(own_keys[0], (NODES, F), 1.0, 6.0, ((0, 16),))
    order_weights = scatter_about(key_of[1], (3, F, F), (3 * F) ** -0.5, 0.15625)
    laplacian_blocks = scatter_about(own_keys[2], (N_BLK, N_REP, N_BLK, CAP, TILE, TILE), (N_BLK * N_REP * TILE * 3 // 5) ** -0.5, 0.15625, ((0, 4), (1, 4)))
    tile_place = draw_tile_place(jax.random.fold_in(jax.random.fold_in(key_of[5], part), 71), part)
    tile_count = draw_tile_count(jax.random.fold_in(jax.random.fold_in(key_of[5], part), 71), part)
    return dict(features=features, order_weights=order_weights, laplacian_blocks=laplacian_blocks, tile_place=tile_place, tile_count=tile_count)


def lane_rows(lane_feats, block_entries, places, counts):
    selected_rows = lane_feats[jnp.arange(N_BLK)[:, None], places % COLT]
    products = jnp.einsum('jcab,jcbf->jcaf', block_entries.astype(jnp.float32), selected_rows.astype(jnp.float32), precision=lax.Precision.HIGHEST)
    live_mask = jnp.arange(CAP)[None, :] < counts[:, None]
    hits = ((places // COLT)[..., None] == jnp.arange(ROWT)[None, None, :]) & live_mask[..., None]
    row_selection = jnp.where(hits, 1.0, 0.0).astype(jnp.float32)
    return jnp.einsum('jcr,jcaf->raf', row_selection, products, precision=lax.Precision.HIGHEST)


def apply_lap(feats, laplacian_blocks, tile_place, tile_count):
    lanes = feats.reshape(N_BLK, N_REP, COLT, TILE, F).transpose(1, 0, 2, 3, 4)
    tiles_flat = laplacian_blocks.reshape(N_BLK * N_REP, N_BLK, CAP, TILE, TILE)
    place_flat = tile_place.reshape(N_BLK * N_REP, N_BLK, CAP)
    count_flat = tile_count.reshape(N_BLK * N_REP, N_BLK)
    lane_ids = (jnp.arange(N_BLK * N_REP) % N_REP).astype(jnp.int32)

    def one_lane(item):
        block_entries, places, counts, lane_number = item
        lane_feats = lax.dynamic_index_in_dim(lanes, lane_number, 0, keepdims=False)
        return lane_rows(lane_feats, block_entries, places, counts)

    pieces = lax.map(one_lane, (tiles_flat, place_flat, count_flat, lane_ids))
    return pieces.reshape(N_BLK, N_REP, STRIP, F).sum(axis=1).reshape(NODES, F)


def reference(features, order_weights, laplacian_blocks, tile_place, tile_count):
    first = apply_lap(features, laplacian_blocks, tile_place, tile_count).astype(jnp.bfloat16)
    second_sum = apply_lap(first, laplacian_blocks, tile_place, tile_count)
    second = (2.0 * second_sum - features.astype(jnp.float32)).astype(jnp.bfloat16)
    stacked = jnp.concatenate([features, first, second], axis=1)
    mixed = jnp.dot(stacked, order_weights.reshape(3 * F, F), preferred_element_type=jnp.float32)
    return mixed.astype(jnp.bfloat16)
```

```python
import functools

import jax
import jax.numpy as jnp
from jax import lax
from jax.experimental import pallas as pl
from jax.experimental.pallas import tpu as pltpu
from jax.sharding import PartitionSpec as P

BF16 = jnp.bfloat16
F32 = jnp.float32


def swap(array, axis, mask):
    peers = lax.axis_size(axis)
    return lax.ppermute(array, axis, [(i, i ^ mask) for i in range(peers)])


def call(kernel, out_shapes, *args, scalars=0, scratch=(), vmem=None, flops=0):
    smem = pl.BlockSpec(memory_space=pltpu.SMEM)
    whole = pl.BlockSpec(memory_space=pltpu.VMEM)
    size = sum(a.size * a.dtype.itemsize for a in args)
    return pl.pallas_call(
        kernel,
        out_shape=out_shapes,
        in_specs=[smem] * scalars + [whole] * (len(args) - scalars),
        out_specs=jax.tree.map(lambda _: whole, out_shapes),
        scratch_shapes=list(scratch),
        compiler_params=pltpu.CompilerParams(vmem_limit_bytes=vmem or (16 << 20)),
        cost_estimate=pl.CostEstimate(flops=flops, bytes_accessed=size, transcendentals=0),
    )(*args)


def dense_kernel(where_ref, place_ref, count_ref, blocks_ref, dense_ref):
    n_blk, cap, tile, _ = blocks_ref.shape
    own = where_ref[0]
    dense_ref[...] = jnp.zeros_like(dense_ref)
    for m in range(n_blk):
        j = own ^ m
        for slot in range(cap):

            @pl.when(slot < count_ref[j])
            def _():
                row = pl.multiple_of(place_ref[j, slot] * tile, tile)
                dense_ref[pl.ds(row, tile), m * tile : (m + 1) * tile] = blocks_ref[j, slot]


def dot(a, b):
    return jnp.dot(a, b, preferred_element_type=F32)


def first_kernel(n_blk, n_rep, tile, *refs):
    lanes, refs = refs[:n_rep], refs[n_rep:]
    pieces, out_ref = refs[:-1], refs[-1]
    chips = n_rep // 2
    total = None
    for m in range(n_blk):
        for k in range(n_rep):
            part = dot(lanes[k][:, m * tile : (m + 1) * tile], pieces[m * chips + k // 2][k % 2])
            total = part if total is None else total + part
    out_ref[...] = total.astype(BF16)


def second_kernel(n_blk, n_rep, tile, where_ref, *refs):
    lanes, refs = refs[:n_rep], refs[n_rep:]
    firsts, refs = refs[:n_blk], refs[n_blk:]
    chips = n_rep // 2
    feats, out_ref, total_ref = refs[:chips], refs[chips], refs[chips + 1]
    rep = where_ref[1]
    total = None
    for m in range(n_blk):
        for k in range(n_rep):
            rows = pl.ds(pl.multiple_of((rep ^ k) * tile, tile), tile)
            part = dot(lanes[k][:, m * tile : (m + 1) * tile], firsts[m][rows, :])
            total = part if total is None else total + part
    total_ref[...] = total
    for k in range(n_rep):
        rows = pl.ds(pl.multiple_of((rep ^ k) * tile, tile), tile)
        out_ref[rows, :] = (2.0 * total_ref[rows, :] - feats[k // 2][k % 2].astype(F32)).astype(BF16)


def weigh(rep, n_rep, near_ref, far_ref, weight_ref, order):
    chips, _, width = near_ref.shape
    total = None
    for k in range(n_rep):
        lane = rep ^ k
        at = (lane % 2) * chips + lane // 2
        rows = pl.ds(pl.multiple_of(at * width, width), width)
        piece = far_ref[k // 2] if k % 2 else near_ref[k // 2]
        part = dot(piece, weight_ref[order, rows, :])
        total = part if total is None else total + part
    return total


def early_kernel(n_rep, where_ref, feats_ref, near_ref, far_ref, weight_ref, out_ref):
    total = dot(feats_ref[...], weight_ref[0])
    out_ref[...] = total + weigh(where_ref[1], n_rep, near_ref, far_ref, weight_ref, 1)


def last_kernel(n_rep, where_ref, early_ref, near_ref, far_ref, weight_ref, out_ref):
    total = early_ref[...] + weigh(where_ref[1], n_rep, near_ref, far_ref, weight_ref, 2)
    out_ref[...] = total.astype(BF16)


def to_owners(strip, rep, n_rep, tile):
    chips = n_rep // 2
    x, c = rep // 2, rep % 2
    got = []
    for i in range(chips):
        rows = lax.dynamic_slice_in_dim(strip, (x ^ i) * 2 * tile, 2 * tile, 0)
        got.append(swap(rows, "rep", 2 * i) if i else rows)
    got = jnp.stack(got).reshape(chips, 2, tile, strip.shape[1])
    near = lax.dynamic_index_in_dim(got, c, 1, keepdims=False)
    far = swap(lax.dynamic_index_in_dim(got, 1 - c, 1, keepdims=False), "rep", 1)
    return near, far


def per_device(features, order_weights, laplacian_blocks, tile_place, tile_count):
    n_blk, n_rep = lax.axis_size("blk"), lax.axis_size("rep")
    blk, rep = lax.axis_index("blk"), lax.axis_index("rep")
    chips = n_rep // 2
    x, c = rep // 2, rep % 2
    tile, feat = features.shape
    strip = n_rep * tile
    width = feat // n_rep
    half = feat // 2
    where = jnp.stack([blk, rep]).astype(jnp.int32)
    vmem = max(16 << 20, int(1.25 * (strip * n_blk * strip + 4 * n_blk * strip * 128) * 2) + (12 << 20))

    kept = lax.dynamic_slice_in_dim(features, c * half, half, 1)
    given = lax.dynamic_slice_in_dim(features, (1 - c) * half, half, 1)
    chip_rows = jnp.stack([kept, swap(given, "rep", 1)])
    pieces = []
    for i in range(chips):
        piece = lax.dynamic_slice_in_dim(chip_rows, (x ^ i) * width, width, 2)
        pieces.append(swap(piece, "rep", 2 * i) if i else piece)

    dense = call(
        dense_kernel,
        jax.ShapeDtypeStruct((strip, n_blk * tile), BF16),
        where, tile_place[0, 0], tile_count[0, 0], laplacian_blocks[0, 0],
        scalars=3, vmem=vmem,
    )
    lanes = []
    for i in range(chips):
        got = swap(dense, "rep", 2 * i) if i else dense
        lanes += [got, swap(got, "rep", 1)]

    gathered = []
    for m in range(n_blk):
        gathered += [swap(piece, "blk", m) if m else piece for piece in pieces]
    strip_shape = jax.ShapeDtypeStruct((strip, width), BF16)
    macs = 2 * strip * n_blk * strip * width
    first = call(
        functools.partial(first_kernel, n_blk, n_rep, tile), strip_shape, *lanes, *gathered,
        vmem=vmem, flops=macs,
    )
    firsts = [swap(first, "blk", m) if m else first for m in range(n_blk)]
    early_near, early_far = to_owners(first, rep, n_rep, tile)
    early = call(
        functools.partial(early_kernel, n_rep),
        jax.ShapeDtypeStruct((tile, feat), F32),
        where, features, early_near, early_far, order_weights,
        scalars=1,
    )
    second = call(
        functools.partial(second_kernel, n_blk, n_rep, tile), strip_shape, where, *lanes, *firsts, *pieces,
        scalars=1, scratch=[pltpu.VMEM((strip, width), F32)], vmem=vmem, flops=macs,
    )
    near, far = to_owners(second, rep, n_rep, tile)
    return call(
        functools.partial(last_kernel, n_rep),
        jax.ShapeDtypeStruct((tile, feat), BF16),
        where, early, near, far, order_weights,
        scalars=1,
    )


def solution(mesh):
    in_specs = (
        P(("groups", "blk", "rep"), None),
        P(),
        P(("groups", "blk"), "rep", None, None, None, None),
        P(("groups", "blk"), "rep", None, None),
        P(("groups", "blk"), "rep", None),
    )
    out_specs = P(("groups", "blk", "rep"), None)
    return jax.shard_map(
        per_device, mesh=mesh, in_specs=in_specs, out_specs=out_specs, check_vma=False
    )
```

```python
import functools

import jax
import jax.numpy as jnp
from jax import lax
from jax.experimental import pallas as pl
from jax.experimental.pallas import tpu as pltpu
from jax.sharding import PartitionSpec as P

BF16 = jnp.bfloat16
F32 = jnp.float32
MIB = 1 << 20


def swap(array, axis, mask):
    peers = lax.axis_size(axis)
    return lax.ppermute(array, axis, [(i, i ^ mask) for i in range(peers)])


def near_by(array):
    if array.size * array.dtype.itemsize > MIB:
        return array
    return pltpu.with_memory_space_constraint(array, pltpu.VMEM)


def after(values, *earlier):
    left = pl.BlockSpec(memory_space=pl.ANY)
    return pl.pallas_call(
        lambda *refs: None,
        out_shape=[jax.ShapeDtypeStruct(v.shape, v.dtype) for v in values],
        in_specs=[left] * (len(values) + len(earlier)),
        out_specs=[left] * len(values),
        input_output_aliases={i: i for i in range(len(values))},
        compiler_params=pltpu.CompilerParams(vmem_limit_bytes=MIB),
    )(*values, *[near_by(e) for e in earlier])


def call(kernel, out_shapes, *args, scalars=0, scratch=(), vmem=4 * MIB, flops=0, hbm=0, earlier=()):
    smem = pl.BlockSpec(memory_space=pltpu.SMEM)
    whole = pl.BlockSpec(memory_space=pltpu.VMEM)
    left = pl.BlockSpec(memory_space=pl.ANY)
    home = pl.BlockSpec(memory_space=pltpu.HBM)
    size = sum(a.size * a.dtype.itemsize for a in args)
    first_whole = scalars + hbm
    n_args, n_all = len(args), len(args) + len(earlier)

    def body(*refs):
        kernel(*refs[:n_args], *refs[n_all:])

    return pl.pallas_call(
        body,
        out_shape=out_shapes,
        in_specs=[smem] * scalars + [home] * hbm + [whole] * (n_args - scalars - hbm) + [left] * len(earlier),
        out_specs=jax.tree.map(lambda _: whole, out_shapes),
        scratch_shapes=list(scratch),
        compiler_params=pltpu.CompilerParams(vmem_limit_bytes=vmem),
        cost_estimate=pl.CostEstimate(flops=flops, bytes_accessed=size, transcendentals=0),
    )(*args[:first_whole], *[near_by(a) for a in (*args[first_whole:], *earlier)])


def dense_kernel(where_ref, place_hbm, count_hbm, blocks_hbm, *refs):
    halves, (place_ref, count_ref, blocks_ref, sems) = refs[:-4], refs[-4:]
    n_blk, cap, tile = blocks_ref.shape[2:5]
    copies = [
        pltpu.make_async_copy(blocks_hbm, blocks_ref, sems.at[0]),
        pltpu.make_async_copy(place_hbm, place_ref, sems.at[1]),
        pltpu.make_async_copy(count_hbm, count_ref, sems.at[2]),
    ]
    for copy in copies:
        copy.start()
    for half in halves:
        half[...] = jnp.zeros_like(half)
    own = where_ref[0]
    for copy in copies:
        copy.wait()
    each = n_blk // len(halves)
    for m in range(n_blk):
        j = own ^ m
        out_ref, at = halves[m // each], (m % each) * tile
        for slot in range(cap):

            @pl.when(slot < count_ref[0, 0, j])
            def _():
                row = pl.multiple_of(place_ref[0, 0, j, slot] * tile, tile)
                out_ref[pl.ds(row, tile), at : at + tile] = blocks_ref[0, 0, j, slot]


def dot(a, b):
    return jnp.dot(a, b, preferred_element_type=F32)


def apply_lanes(lanes, n_blk, tile, rows_of):
    total = None
    each = n_blk // len(lanes[0])
    for m in range(n_blk):
        at = (m % each) * tile
        left = jnp.concatenate([halves[m // each][:, at : at + tile] for halves in lanes], axis=1)
        right = jnp.concatenate([rows_of(m, k) for k in range(len(lanes))], axis=0)
        part = dot(left, right)
        total = part if total is None else total + part
    return total


def paired(refs, n):
    return [refs[i : i + n] for i in range(0, len(refs), n)]


def part_kernel(n_blk, tile, masks, *refs):
    n = len(masks)
    lanes, pieces, more, out_ref = paired(refs[:n], 1), refs[n : n + n_blk], refs[n + n_blk : -1], refs[-1]
    total = apply_lanes(lanes, n_blk, tile, lambda m, i: pieces[m][masks[i] // 2, masks[i] % 2])
    if more:
        total = total + more[0][...]
    out_ref[...] = total.astype(out_ref.dtype)


def second_kernel(n_blk, n_half, n_rep, tile, where_ref, *refs):
    lanes, refs = paired(refs[: n_rep * n_half], n_half), refs[n_rep * n_half :]
    firsts, feats, out_ref, total_ref = refs[:n_blk], refs[n_blk], refs[n_blk + 1], refs[n_blk + 2]
    rep = where_ref[1]

    def rows(k):
        return pl.ds(pl.multiple_of((rep ^ k) * tile, tile), tile)

    total_ref[...] = apply_lanes(lanes, n_blk, tile, lambda m, k: firsts[m][rows(k), :])
    for k in range(n_rep):
        out_ref[rows(k), :] = (2.0 * total_ref[rows(k), :] - feats[k // 2, k % 2].astype(F32)).astype(BF16)


def weigh(rep, n_rep, near_ref, far_ref, weight_ref, order):
    chips, _, width = near_ref.shape
    total = None
    for k in range(n_rep):
        lane = rep ^ k
        at = (lane % 2) * chips + lane // 2
        rows = pl.ds(pl.multiple_of(at * width, width), width)
        piece = far_ref[k // 2] if k % 2 else near_ref[k // 2]
        part = dot(piece, weight_ref[order, rows, :])
        total = part if total is None else total + part
    return total


def early_kernel(n_rep, where_ref, feats_ref, near_ref, far_ref, weight_ref, out_ref):
    total = dot(feats_ref[...], weight_ref[0])
    out_ref[...] = total + weigh(where_ref[1], n_rep, near_ref, far_ref, weight_ref, 1)


def last_kernel(n_rep, where_ref, early_ref, near_ref, far_ref, weight_ref, out_ref):
    total = early_ref[...] + weigh(where_ref[1], n_rep, near_ref, far_ref, weight_ref, 2)
    out_ref[...] = total.astype(BF16)


def to_owners(parts, rep, n_rep):
    c = rep % 2
    got = jnp.stack([swap(part, "rep", 2 * i) if i else part for i, part in enumerate(parts)])
    got = got.reshape(got.shape[0], 2, -1, got.shape[2])
    near = lax.dynamic_index_in_dim(got, c, 1, keepdims=False)
    far = swap(lax.dynamic_index_in_dim(got, 1 - c, 1, keepdims=False), "rep", 1)
    return near, far


def by_chip(strip, rep, n_rep):
    size = strip.shape[0] * 2 // n_rep
    return [lax.dynamic_slice_in_dim(strip, ((rep // 2) ^ i) * size, size, 0) for i in range(n_rep // 2)]


def per_device(features, order_weights, laplacian_blocks, tile_place, tile_count):
    n_blk, n_rep = lax.axis_size("blk"), lax.axis_size("rep")
    blk, rep = lax.axis_index("blk"), lax.axis_index("rep")
    chips = n_rep // 2
    x, c = rep // 2, rep % 2
    tile, feat = features.shape
    strip = n_rep * tile
    width = feat // n_rep
    half = feat // 2
    n_half = 1
    where = jnp.stack([blk, rep]).astype(jnp.int32)
    lane_bytes = 2 * strip * n_blk * tile
    rows_bytes = 2 * strip * n_blk * max(width, 128)

    kept = lax.dynamic_slice_in_dim(features, c * half, half, 1)
    given = lax.dynamic_slice_in_dim(features, (1 - c) * half, half, 1)
    got = swap(given, "rep", 1)
    chip_rows = jnp.stack([kept, got])
    half_shape = jax.ShapeDtypeStruct((strip, n_blk // n_half * tile), BF16)
    dense = call(
        dense_kernel,
        half_shape,
        where,
        *(pltpu.with_memory_space_constraint(a, pltpu.HBM) for a in (tile_place, tile_count, laplacian_blocks)),
        scalars=1,
        hbm=3,
        vmem=3 * lane_bytes + 2 * MIB,
        scratch=[
            pltpu.SMEM(tile_place.shape, jnp.int32),
            pltpu.SMEM(tile_count.shape, jnp.int32),
            pltpu.VMEM(laplacian_blocks.shape, BF16),
            pltpu.SemaphoreType.DMA((3,)),
        ],
    )
    own_chip = [dense, swap(dense, "rep", 1)]

    pieces = []
    for i in range(chips):
        piece = lax.dynamic_slice_in_dim(chip_rows, (x ^ i) * width, width, 2)
        pieces.append(swap(piece, "rep", 2 * i) if i else piece)
    own_rows = jnp.stack(pieces)
    rows = [swap(own_rows, "blk", m) if m else own_rows for m in range(n_blk)]
    arrived = [swap(after([dense], pieces[i])[0], "rep", 2 * i) for i in range(1, chips)]
    tied = after([*rows[1:], *arrived])
    rows, arrived = [own_rows, *tied[: n_blk - 1]], tied[n_blk - 1 :]
    lanes = [*own_chip]
    for got in arrived:
        lanes += [got, swap(got, "rep", 1)]

    strip_shape = jax.ShapeDtypeStruct((strip, width), BF16)
    vmem = n_rep * lane_bytes + 2 * rows_bytes + 4 * MIB
    macs = 2 * strip * n_blk * strip * width
    soon = [0, 1, *range(2, n_rep, 2)]
    late = [*range(3, n_rep, 2)]
    part = call(
        functools.partial(part_kernel, n_blk, tile, soon), jax.ShapeDtypeStruct((strip, width), F32),
        *[lanes[k] for k in soon], *rows,
        vmem=vmem, flops=macs,
    )
    first = call(
        functools.partial(part_kernel, n_blk, tile, late), strip_shape,
        *[lanes[k] for k in late], *rows, part,
        vmem=vmem, flops=macs,
    )
    firsts = [swap(first, "blk", m) for m in range(1, n_blk)]
    tied = after([*firsts, *by_chip(first, rep, n_rep)])
    firsts, first_parts = [first, *tied[: n_blk - 1]], tied[n_blk - 1 :]
    early_near, early_far = to_owners(first_parts, rep, n_rep)
    early = call(
        functools.partial(early_kernel, n_rep),
        jax.ShapeDtypeStruct((tile, feat), F32),
        where, features, early_near, early_far, order_weights,
        scalars=1,
    )
    second = call(
        functools.partial(second_kernel, n_blk, n_half, n_rep, tile), strip_shape,
        where, *lanes, *firsts, own_rows,
        scalars=1, vmem=vmem, flops=macs,
        scratch=[pltpu.VMEM((strip, width), F32)],
    )
    near, far = to_owners(by_chip(second, rep, n_rep), rep, n_rep)
    return call(
        functools.partial(last_kernel, n_rep),
        jax.ShapeDtypeStruct((tile, feat), BF16),
        where, early, near, far, order_weights,
        scalars=1,
    )


def solution(mesh):
    in_specs = (
        P(("groups", "blk", "rep"), None),
        P(),
        P(("groups", "blk"), "rep", None, None, None, None),
        P(("groups", "blk"), "rep", None, None),
        P(("groups", "blk"), "rep", None),
    )
    out_specs = P(("groups", "blk", "rep"), None)
    return jax.shard_map(
        per_device, mesh=mesh, in_specs=in_specs, out_specs=out_specs, check_vma=False
    )
```

```python
import functools

import jax
import jax.numpy as jnp
from jax import lax
from jax.experimental import pallas as pl
from jax.experimental.pallas import tpu as pltpu
from jax.sharding import PartitionSpec as P

BF16 = jnp.bfloat16
F32 = jnp.float32
MIB = 1 << 20


def swap(array, axis, mask):
    peers = lax.axis_size(axis)
    return lax.ppermute(array, axis, [(i, i ^ mask) for i in range(peers)])


def near_by(array):
    if array.size * array.dtype.itemsize > MIB:
        return array
    return pltpu.with_memory_space_constraint(array, pltpu.VMEM)


def after(values, *earlier):
    left = pl.BlockSpec(memory_space=pl.ANY)
    return pl.pallas_call(
        lambda *refs: None,
        out_shape=[jax.ShapeDtypeStruct(v.shape, v.dtype) for v in values],
        in_specs=[left] * (len(values) + len(earlier)),
        out_specs=[left] * len(values),
        input_output_aliases={i: i for i in range(len(values))},
        compiler_params=pltpu.CompilerParams(vmem_limit_bytes=MIB),
    )(*values, *[near_by(e) for e in earlier])


def call(kernel, out_shapes, *args, scratch=(), vmem=4 * MIB, flops=0, hbm=0, earlier=()):
    whole = pl.BlockSpec(memory_space=pltpu.VMEM)
    left = pl.BlockSpec(memory_space=pl.ANY)
    home = pl.BlockSpec(memory_space=pltpu.HBM)
    size = sum(a.size * a.dtype.itemsize for a in args)
    n_args, n_all = len(args), len(args) + len(earlier)

    def body(*refs):
        kernel(*refs[:n_args], *refs[n_all:])

    return pl.pallas_call(
        body,
        out_shape=out_shapes,
        in_specs=[home] * hbm + [whole] * (n_args - hbm) + [left] * len(earlier),
        out_specs=jax.tree.map(lambda _: whole, out_shapes),
        scratch_shapes=list(scratch),
        compiler_params=pltpu.CompilerParams(vmem_limit_bytes=vmem),
        cost_estimate=pl.CostEstimate(flops=flops, bytes_accessed=size, transcendentals=0),
    )(*args[:hbm], *[near_by(a) for a in (*args[hbm:], *earlier)])


def dense_kernel(place_hbm, count_hbm, blocks_hbm, feats_hbm, dense_ref, cut_ref, *scratch):
    place_ref, count_ref, blocks_ref, feats_ref, sems = scratch
    n_blk, cap, tile = blocks_ref.shape[2:5]
    chips, width = cut_ref.shape[0], cut_ref.shape[2]
    pairs = [(blocks_hbm, blocks_ref), (place_hbm, place_ref), (count_hbm, count_ref), (feats_hbm, feats_ref)]
    copies = [pltpu.make_async_copy(a, b, sems.at[i]) for i, (a, b) in enumerate(pairs)]
    for copy in copies:
        copy.start()
    dense_ref[...] = jnp.zeros_like(dense_ref)
    own, rep = lax.axis_index("blk"), lax.axis_index("rep")
    for copy in copies:
        copy.wait()
    for i in range(chips):
        if width % 128 == 0:
            cut_ref[i] = feats_ref[:, pl.ds(pl.multiple_of((rep ^ 2 * i) * width, width), width)]
        else:
            for lane in range(feats_ref.shape[1] // width):

                @pl.when(lane == rep ^ 2 * i)
                def _():
                    cut_ref[i] = feats_ref[:, lane * width : (lane + 1) * width]

    for m in range(n_blk):
        j = own ^ m
        at = m * tile
        for slot in range(cap):

            @pl.when(slot < count_ref[0, 0, j])
            def _():
                row = pl.multiple_of(place_ref[0, 0, j, slot] * tile, tile)
                dense_ref[pl.ds(row, tile), at : at + tile] = blocks_ref[0, 0, j, slot]


def dot(a, b):
    return jnp.dot(a, b, preferred_element_type=F32)


def apply_lanes(lanes, n_blk, tile, rows_of):
    total = None
    each = n_blk // len(lanes[0])
    for m in range(n_blk):
        at = (m % each) * tile
        left = jnp.concatenate([halves[m // each][:, at : at + tile] for halves in lanes], axis=1)
        right = jnp.concatenate([rows_of(m, k) for k in range(len(lanes))], axis=0)
        part = dot(left, right)
        total = part if total is None else total + part
    return total


def paired(refs, n):
    return [refs[i : i + n] for i in range(0, len(refs), n)]


def part_kernel(n_blk, tile, masks, *refs):
    n = len(masks)
    lanes, pieces, more, out_ref = paired(refs[:n], 1), refs[n : n + n_blk], refs[n + n_blk : -1], refs[-1]
    total = apply_lanes(lanes, n_blk, tile, lambda m, i: pieces[m][masks[i] // 2, masks[i] % 2])
    if more:
        total = total + more[0][...]
    out_ref[...] = total.astype(out_ref.dtype)


def second_kernel(n_blk, n_rep, tile, chip, *refs):
    lanes, refs = refs[:n_rep], refs[n_rep:]
    firsts, feats, out_ref, total_ref = refs[:n_blk], refs[n_blk], refs[n_blk + 1], refs[n_blk + 2]
    rep = lax.axis_index("rep")
    size = 2 * tile
    mine = pl.ds(pl.multiple_of((rep // 2 ^ chip) * size, size), size)
    total = None
    for m in range(n_blk):
        left = jnp.concatenate([lane[mine, m * tile : (m + 1) * tile] for lane in lanes], axis=1)
        rows = [pl.ds(pl.multiple_of((rep ^ k) * tile, tile), tile) for k in range(n_rep)]
        part = dot(left, jnp.concatenate([firsts[m][r, :] for r in rows], axis=0))
        total = part if total is None else total + part
    total_ref[...] = total
    for i in range(2):
        rows = pl.ds(pl.multiple_of((rep % 2 ^ i) * tile, tile), tile)
        out_ref[i] = (2.0 * total_ref[rows, :] - feats[chip, i].astype(F32)).astype(BF16)


def weigh(rep, n_rep, near_ref, far_ref, weight_ref, order):
    width = near_ref.shape[2]
    pieces, weights = [], []
    for k in range(n_rep):
        pieces.append(far_ref[k // 2] if k % 2 else near_ref[k // 2])
        weights.append(weight_ref[order, pl.ds(pl.multiple_of((rep ^ k) * width, width), width), :])
    return dot(jnp.concatenate(pieces, axis=1), jnp.concatenate(weights, axis=0))


def early_kernel(n_rep, feats_ref, near_ref, far_ref, weight_ref, out_ref):
    total = dot(feats_ref[...], weight_ref[0])
    out_ref[...] = total + weigh(lax.axis_index("rep"), n_rep, near_ref, far_ref, weight_ref, 1)


def last_kernel(n_rep, early_ref, near_ref, far_ref, weight_ref, out_ref):
    total = early_ref[...] + weigh(lax.axis_index("rep"), n_rep, near_ref, far_ref, weight_ref, 2)
    out_ref[...] = total.astype(BF16)


def to_owners(parts):
    near = jnp.stack([swap(part, "rep", 2 * i) if i else part for i, part in enumerate(parts)])
    return near[:, 0], swap(near[:, 1], "rep", 1)


def per_device(features, order_weights, laplacian_blocks, tile_place, tile_count):
    n_blk, n_rep = lax.axis_size("blk"), lax.axis_size("rep")
    rep = lax.axis_index("rep")
    chips = n_rep // 2
    tile, feat = features.shape
    strip = n_rep * tile
    width = feat // n_rep
    lane_bytes = 2 * strip * n_blk * tile
    rows_bytes = 2 * strip * n_blk * max(width, 128)

    dense, own_cut = call(
        dense_kernel,
        (jax.ShapeDtypeStruct((strip, n_blk * tile), BF16), jax.ShapeDtypeStruct((chips, tile, width), BF16)),
        *(pltpu.with_memory_space_constraint(a, pltpu.HBM) for a in (tile_place, tile_count, laplacian_blocks, features)),
        hbm=4,
        vmem=3 * lane_bytes + 3 * MIB,
        scratch=[
            pltpu.SMEM(tile_place.shape, jnp.int32),
            pltpu.SMEM(tile_count.shape, jnp.int32),
            pltpu.VMEM(laplacian_blocks.shape, BF16),
            pltpu.VMEM(features.shape, BF16),
            pltpu.SemaphoreType.DMA((4,)),
        ],
    )

    got = swap(features, "rep", 1)
    cut = lambda i: jnp.stack([own_cut[i], lax.dynamic_slice_in_dim(got, (rep ^ 2 * i) * width, width, 1)])
    pieces = [swap(cut(i), "rep", 2 * i) if i else cut(i) for i in range(chips)]
    own_rows, mate = after([jnp.stack(pieces), swap(dense, "rep", 1)])
    own_chip = [dense, mate]
    rows = [swap(own_rows, "blk", m) if m else own_rows for m in range(n_blk)]
    arrived = [swap(after([dense], pieces[i])[0], "rep", 2 * i) for i in range(1, chips)]
    lanes = [*own_chip]
    for got in arrived:
        lanes += [got, swap(got, "rep", 1)]

    strip_shape = jax.ShapeDtypeStruct((strip, width), BF16)
    vmem = n_rep * lane_bytes + 2 * rows_bytes + 4 * MIB
    macs = 2 * strip * n_blk * strip * width
    soon = [0, 1, *range(2, n_rep, 2)]
    late = [*range(3, n_rep, 2)]
    part = call(
        functools.partial(part_kernel, n_blk, tile, soon), jax.ShapeDtypeStruct((strip, width), F32),
        *[lanes[k] for k in soon], *rows,
        vmem=vmem, flops=1 << 35,
    )
    first = call(
        functools.partial(part_kernel, n_blk, tile, late), strip_shape,
        *[lanes[k] for k in late], *rows, part,
        vmem=vmem, flops=macs,
    )
    firsts = [swap(first, "blk", m) for m in range(1, n_blk)]
    lane_rows = lambda k: lax.dynamic_slice_in_dim(first, (rep ^ k) * tile, tile, 0)
    parts = [jnp.stack([lane_rows(2 * i), lane_rows(2 * i + 1)]) for i in range(chips)]
    tied = after([*firsts, *parts])
    firsts, parts = [first, *tied[: n_blk - 1]], tied[n_blk - 1 :]
    early_near, early_far = to_owners(parts)
    early = call(
        functools.partial(early_kernel, n_rep),
        jax.ShapeDtypeStruct((tile, feat), F32),
        features, early_near, early_far, order_weights,
    )
    parts = [None] * chips
    for i in [*range(1, chips), 0]:
        parts[i] = call(
            functools.partial(second_kernel, n_blk, n_rep, tile, i),
            jax.ShapeDtypeStruct((2, tile, width), BF16),
            *lanes, *firsts, own_rows,
            vmem=vmem, flops=2 * macs // n_rep,
            scratch=[pltpu.VMEM((2 * tile, width), F32)],
        )
    near, far = to_owners(parts)
    return call(
        functools.partial(last_kernel, n_rep),
        jax.ShapeDtypeStruct((tile, feat), BF16),
        early, near, far, order_weights,
    )


def solution(mesh):
    in_specs = (
        P(("groups", "blk", "rep"), None),
        P(),
        P(("groups", "blk"), "rep", None, None, None, None),
        P(("groups", "blk"), "rep", None, None),
        P(("groups", "blk"), "rep", None),
    )
    out_specs = P(("groups", "blk", "rep"), None)
    return jax.shard_map(
        per_device, mesh=mesh, in_specs=in_specs, out_specs=out_specs, check_vma=False
    )
```

```python
import functools

import jax
import jax.numpy as jnp
from jax import lax
from jax.experimental import pallas as pl
from jax.experimental.pallas import tpu as pltpu
from jax.sharding import PartitionSpec as P

BF16 = jnp.bfloat16
F32 = jnp.float32
MIB = 1 << 20


def swap(array, axis, mask):
    peers = lax.axis_size(axis)
    return lax.ppermute(array, axis, [(i, i ^ mask) for i in range(peers)])


def near_by(array):
    if array.size * array.dtype.itemsize > MIB:
        return array
    return pltpu.with_memory_space_constraint(array, pltpu.VMEM)


def after(values, *earlier):
    left = pl.BlockSpec(memory_space=pl.ANY)
    return pl.pallas_call(
        lambda *refs: None,
        out_shape=[jax.ShapeDtypeStruct(v.shape, v.dtype) for v in values],
        in_specs=[left] * (len(values) + len(earlier)),
        out_specs=[left] * len(values),
        input_output_aliases={i: i for i in range(len(values))},
        compiler_params=pltpu.CompilerParams(vmem_limit_bytes=MIB),
    )(*values, *[near_by(e) for e in earlier])


def call(kernel, out_shapes, *args, scratch=(), vmem=4 * MIB, flops=0, hbm=0, earlier=()):
    whole = pl.BlockSpec(memory_space=pltpu.VMEM)
    left = pl.BlockSpec(memory_space=pl.ANY)
    home = pl.BlockSpec(memory_space=pltpu.HBM)
    size = sum(a.size * a.dtype.itemsize for a in args)
    n_args, n_all = len(args), len(args) + len(earlier)

    def body(*refs):
        kernel(*refs[:n_args], *refs[n_all:])

    return pl.pallas_call(
        body,
        out_shape=out_shapes,
        in_specs=[home] * hbm + [whole] * (n_args - hbm) + [left] * len(earlier),
        out_specs=jax.tree.map(lambda _: whole, out_shapes),
        scratch_shapes=list(scratch),
        compiler_params=pltpu.CompilerParams(vmem_limit_bytes=vmem),
        cost_estimate=pl.CostEstimate(flops=flops, bytes_accessed=size, transcendentals=0),
    )(*args[:hbm], *[near_by(a) for a in (*args[hbm:], *earlier)])


def dense_kernel(place_hbm, count_hbm, blocks_hbm, feats_hbm, dense_ref, cut_ref, *scratch):
    place_ref, count_ref, blocks_ref, feats_ref, sems = scratch
    n_blk, cap, tile = blocks_ref.shape[2:5]
    chips, width = cut_ref.shape[0], cut_ref.shape[2]
    pairs = [(blocks_hbm, blocks_ref), (place_hbm, place_ref), (count_hbm, count_ref), (feats_hbm, feats_ref)]
    copies = [pltpu.make_async_copy(a, b, sems.at[i]) for i, (a, b) in enumerate(pairs)]
    for copy in copies:
        copy.start()
    dense_ref[...] = jnp.zeros_like(dense_ref)
    own, rep = lax.axis_index("blk"), lax.axis_index("rep")
    for copy in copies:
        copy.wait()
    for i in range(chips):
        if width % 128 == 0:
            cut_ref[i] = feats_ref[:, pl.ds(pl.multiple_of((rep ^ 2 * i) * width, width), width)]
        else:
            for lane in range(feats_ref.shape[1] // width):

                @pl.when(lane == rep ^ 2 * i)
                def _():
                    cut_ref[i] = feats_ref[:, lane * width : (lane + 1) * width]

    for m in range(n_blk):
        j = own ^ m
        at = m * tile
        for slot in range(cap):

            @pl.when(slot < count_ref[0, 0, j])
            def _():
                row = pl.multiple_of(place_ref[0, 0, j, slot] * tile, tile)
                dense_ref[pl.ds(row, tile), at : at + tile] = blocks_ref[0, 0, j, slot]


def dot(a, b):
    return jnp.dot(a, b, preferred_element_type=F32)


def apply_lanes(lanes, n_blk, tile, rows_of):
    total = None
    each = n_blk // len(lanes[0])
    for m in range(n_blk):
        at = (m % each) * tile
        left = jnp.concatenate([halves[m // each][:, at : at + tile] for halves in lanes], axis=1)
        right = jnp.concatenate([rows_of(m, k) for k in range(len(lanes))], axis=0)
        part = dot(left, right)
        total = part if total is None else total + part
    return total


def paired(refs, n):
    return [refs[i : i + n] for i in range(0, len(refs), n)]


def part_kernel(n_blk, tile, masks, *refs):
    n = len(masks)
    lanes, pieces, more, out_ref = paired(refs[:n], 1), refs[n : n + n_blk], refs[n + n_blk : -1], refs[-1]
    total = apply_lanes(lanes, n_blk, tile, lambda m, i: pieces[m][masks[i] // 2, masks[i] % 2])
    if more:
        total = total + more[0][...]
    out_ref[...] = total.astype(out_ref.dtype)


def second_kernel(n_blk, n_rep, tile, *refs):
    lanes, refs = paired(refs[:n_rep], 1), refs[n_rep:]
    firsts, feats, outs, total_ref = refs[:n_blk], refs[n_blk], refs[n_blk + 1 : -1], refs[-1]
    rep = lax.axis_index("rep")
    rows = [pl.ds(pl.multiple_of((rep ^ k) * tile, tile), tile) for k in range(n_rep)]
    total_ref[...] = apply_lanes(lanes, n_blk, tile, lambda m, k: firsts[m][rows[k], :])
    for k, out_ref in enumerate(outs):
        out_ref[0] = firsts[0][rows[k], :]
        out_ref[1] = (2.0 * total_ref[rows[k], :] - feats[k // 2, k % 2].astype(F32)).astype(BF16)


def weigh(pieces, weight_ref, order):
    rep, width = lax.axis_index("rep"), pieces[0].shape[1]
    rows = [pl.ds(pl.multiple_of((rep ^ k) * width, width), width) for k in range(len(pieces))]
    weights = [weight_ref[order, r, :] for r in rows]
    return dot(jnp.concatenate(pieces, axis=1), jnp.concatenate(weights, axis=0))


def early_kernel(feats_ref, weight_ref, out_ref):
    out_ref[...] = dot(feats_ref[...], weight_ref[0])


def last_kernel(early_ref, weight_ref, *refs):
    pieces, out_ref = refs[:-1], refs[-1]
    total = early_ref[...]
    for i in range(2):
        total = total + weigh([piece[i] for piece in pieces], weight_ref, 1 + i)
    out_ref[...] = total.astype(BF16)


def per_device(features, order_weights, laplacian_blocks, tile_place, tile_count):
    n_blk, n_rep = lax.axis_size("blk"), lax.axis_size("rep")
    rep = lax.axis_index("rep")
    chips = n_rep // 2
    tile, feat = features.shape
    strip = n_rep * tile
    width = feat // n_rep
    lane_bytes = 2 * strip * n_blk * tile
    rows_bytes = 2 * strip * n_blk * max(width, 128)

    dense, own_cut = call(
        dense_kernel,
        (jax.ShapeDtypeStruct((strip, n_blk * tile), BF16), jax.ShapeDtypeStruct((chips, tile, width), BF16)),
        *(pltpu.with_memory_space_constraint(a, pltpu.HBM) for a in (tile_place, tile_count, laplacian_blocks, features)),
        hbm=4,
        vmem=3 * lane_bytes + 3 * MIB,
        scratch=[
            pltpu.SMEM(tile_place.shape, jnp.int32),
            pltpu.SMEM(tile_count.shape, jnp.int32),
            pltpu.VMEM(laplacian_blocks.shape, BF16),
            pltpu.VMEM(features.shape, BF16),
            pltpu.SemaphoreType.DMA((4,)),
        ],
    )

    got = swap(features, "rep", 1)
    cut = lambda i: jnp.stack([own_cut[i], lax.dynamic_slice_in_dim(got, (rep ^ 2 * i) * width, width, 1)])
    pieces = [swap(cut(i), "rep", 2 * i) if i else cut(i) for i in range(chips)]
    own_rows, mate = after([jnp.stack(pieces), swap(dense, "rep", 1)])
    own_chip = [dense, mate]
    rows = [swap(own_rows, "blk", m) if m else own_rows for m in range(n_blk)]
    arrived = [swap(after([dense], pieces[i])[0], "rep", 2 * i) for i in range(1, chips)]
    lanes = [*own_chip]
    for got in arrived:
        lanes += [got, swap(got, "rep", 1)]

    strip_shape = jax.ShapeDtypeStruct((strip, width), BF16)
    vmem = n_rep * lane_bytes + 2 * rows_bytes + 4 * MIB
    macs = 2 * strip * n_blk * strip * width
    soon = [0, 1, *range(2, n_rep, 2)]
    late = [*range(3, n_rep, 2)]
    part = call(
        functools.partial(part_kernel, n_blk, tile, soon), jax.ShapeDtypeStruct((strip, width), F32),
        *[lanes[k] for k in soon], *rows,
        vmem=vmem, flops=1 << 35,
    )
    first = call(
        functools.partial(part_kernel, n_blk, tile, late), strip_shape,
        *[lanes[k] for k in late], *rows, part,
        vmem=vmem, flops=macs,
    )
    firsts = [swap(first, "blk", m) for m in range(1, n_blk)]
    firsts = [first, *firsts]
    seconds = call(
        functools.partial(second_kernel, n_blk, n_rep, tile),
        (jax.ShapeDtypeStruct((2, tile, width), BF16),) * n_rep,
        *lanes, *firsts, own_rows,
        vmem=vmem, flops=macs,
        scratch=[pltpu.VMEM((strip, width), F32)],
    )
    seconds = [swap(rows, "rep", k) if k else rows for k, rows in enumerate(seconds)]
    early = call(early_kernel, jax.ShapeDtypeStruct((tile, feat), F32), features, order_weights)
    return call(last_kernel, jax.ShapeDtypeStruct((tile, feat), BF16), early, order_weights, *seconds)


def solution(mesh):
    in_specs = (
        P(("groups", "blk", "rep"), None),
        P(),
        P(("groups", "blk"), "rep", None, None, None, None),
        P(("groups", "blk"), "rep", None, None),
        P(("groups", "blk"), "rep", None),
    )
    out_specs = P(("groups", "blk", "rep"), None)
    return jax.shard_map(
        per_device, mesh=mesh, in_specs=in_specs, out_specs=out_specs, check_vma=False
    )
```

```python
import functools

import jax
import jax.numpy as jnp
from jax import lax
from jax.experimental import pallas as pl
from jax.experimental.pallas import tpu as pltpu
from jax.sharding import PartitionSpec as P

BF16 = jnp.bfloat16
F32 = jnp.float32
MIB = 1 << 20


def swap(array, axis, mask):
    peers = lax.axis_size(axis)
    return lax.ppermute(array, axis, [(i, i ^ mask) for i in range(peers)])


def near_by(array):
    if array.size * array.dtype.itemsize > MIB:
        return array
    return pltpu.with_memory_space_constraint(array, pltpu.VMEM)


def after(values, *earlier):
    left = pl.BlockSpec(memory_space=pl.ANY)
    return pl.pallas_call(
        lambda *refs: None,
        out_shape=[jax.ShapeDtypeStruct(v.shape, v.dtype) for v in values],
        in_specs=[left] * (len(values) + len(earlier)),
        out_specs=[left] * len(values),
        input_output_aliases={i: i for i in range(len(values))},
        compiler_params=pltpu.CompilerParams(vmem_limit_bytes=MIB),
    )(*values, *[near_by(e) for e in earlier])


def call(kernel, out_shapes, *args, scratch=(), vmem=4 * MIB, flops=0, hbm=0, earlier=()):
    whole = pl.BlockSpec(memory_space=pltpu.VMEM)
    left = pl.BlockSpec(memory_space=pl.ANY)
    home = pl.BlockSpec(memory_space=pltpu.HBM)
    size = sum(a.size * a.dtype.itemsize for a in args)
    n_args, n_all = len(args), len(args) + len(earlier)

    def body(*refs):
        kernel(*refs[:n_args], *refs[n_all:])

    return pl.pallas_call(
        body,
        out_shape=out_shapes,
        in_specs=[home] * hbm + [whole] * (n_args - hbm) + [left] * len(earlier),
        out_specs=jax.tree.map(lambda _: whole, out_shapes),
        scratch_shapes=list(scratch),
        compiler_params=pltpu.CompilerParams(vmem_limit_bytes=vmem),
        cost_estimate=pl.CostEstimate(flops=flops, bytes_accessed=size, transcendentals=0),
    )(*args[:hbm], *[near_by(a) for a in (*args[hbm:], *earlier)])


def dense_kernel(place_hbm, count_hbm, blocks_hbm, feats_hbm, dense_ref, cut_ref, *scratch):
    place_ref, count_ref, blocks_ref, feats_ref, sems = scratch
    n_blk, cap, tile = blocks_ref.shape[2:5]
    chips, width = cut_ref.shape[0], cut_ref.shape[2]
    pairs = [(blocks_hbm, blocks_ref), (place_hbm, place_ref), (count_hbm, count_ref), (feats_hbm, feats_ref)]
    copies = [pltpu.make_async_copy(a, b, sems.at[i]) for i, (a, b) in enumerate(pairs)]
    for copy in copies:
        copy.start()
    dense_ref[...] = jnp.zeros_like(dense_ref)
    own, rep = lax.axis_index("blk"), lax.axis_index("rep")
    for copy in copies:
        copy.wait()
    for i in range(chips):
        if width % 128 == 0:
            cut_ref[i] = feats_ref[:, pl.ds(pl.multiple_of((rep ^ 2 * i) * width, width), width)]
        else:
            for lane in range(feats_ref.shape[1] // width):

                @pl.when(lane == rep ^ 2 * i)
                def _():
                    cut_ref[i] = feats_ref[:, lane * width : (lane + 1) * width]

    for m in range(n_blk):
        j = own ^ m
        at = m * tile
        for slot in range(cap):

            @pl.when(slot < count_ref[0, 0, j])
            def _():
                row = pl.multiple_of(place_ref[0, 0, j, slot] * tile, tile)
                dense_ref[pl.ds(row, tile), at : at + tile] = blocks_ref[0, 0, j, slot]


def dot(a, b):
    return jnp.dot(a, b, preferred_element_type=F32)


def apply_lanes(lanes, n_blk, tile, rows_of):
    total = None
    each = n_blk // len(lanes[0])
    for m in range(n_blk):
        at = (m % each) * tile
        left = jnp.concatenate([halves[m // each][:, at : at + tile] for halves in lanes], axis=1)
        right = jnp.concatenate([rows_of(m, k) for k in range(len(lanes))], axis=0)
        part = dot(left, right)
        total = part if total is None else total + part
    return total


def paired(refs, n):
    return [refs[i : i + n] for i in range(0, len(refs), n)]


def part_kernel(n_blk, tile, masks, *refs):
    n = len(masks)
    lanes, pieces, more, out_ref = paired(refs[:n], 1), refs[n : n + n_blk], refs[n + n_blk : -1], refs[-1]
    total = apply_lanes(lanes, n_blk, tile, lambda m, i: pieces[m][masks[i] // 2, masks[i] % 2])
    if more:
        total = total + more[0][...]
    out_ref[...] = total.astype(out_ref.dtype)


def second_kernel(n_blk, n_rep, tile, *refs):
    lanes, refs = paired(refs[:n_rep], 1), refs[n_rep:]
    firsts, feats, outs, total_ref = refs[:n_blk], refs[n_blk], refs[n_blk + 1 : -1], refs[-1]
    rep = lax.axis_index("rep")
    rows = [pl.ds(pl.multiple_of((rep ^ k) * tile, tile), tile) for k in range(n_rep)]
    total_ref[...] = apply_lanes(lanes, n_blk, tile, lambda m, k: firsts[m][rows[k], :])
    for k, out_ref in enumerate(outs):
        if k < 2:
            out_ref[1] = firsts[0][rows[k], :]
        out_ref[0] = (2.0 * total_ref[rows[k], :] - feats[k // 2, k % 2].astype(F32)).astype(BF16)


def weigh(pieces, weight_ref, order, masks):
    rep, width = lax.axis_index("rep"), pieces[0].shape[1]
    rows = [pl.ds(pl.multiple_of((rep ^ k) * width, width), width) for k in masks]
    weights = [weight_ref[order, r, :] for r in rows]
    return dot(jnp.concatenate(pieces, axis=1), jnp.concatenate(weights, axis=0))


def early_kernel(n_rep, feats_ref, weight_ref, *refs):
    others, out_ref = [ref[...] for ref in refs[:-1]], refs[-1]
    out_ref[...] = dot(feats_ref[...], weight_ref[0]) + weigh(others, weight_ref, 1, range(2, n_rep))


def last_kernel(n_rep, early_ref, weight_ref, *refs):
    pieces, out_ref = refs[:-1], refs[-1]
    total = early_ref[...] + weigh([piece[1] for piece in pieces[:2]], weight_ref, 1, range(2))
    total = total + weigh([piece[0] for piece in pieces], weight_ref, 2, range(n_rep))
    out_ref[...] = total.astype(BF16)


def per_device(features, order_weights, laplacian_blocks, tile_place, tile_count):
    n_blk, n_rep = lax.axis_size("blk"), lax.axis_size("rep")
    rep = lax.axis_index("rep")
    chips = n_rep // 2
    tile, feat = features.shape
    strip = n_rep * tile
    width = feat // n_rep
    lane_bytes = 2 * strip * n_blk * tile
    rows_bytes = 2 * strip * n_blk * max(width, 128)

    dense, own_cut = call(
        dense_kernel,
        (jax.ShapeDtypeStruct((strip, n_blk * tile), BF16), jax.ShapeDtypeStruct((chips, tile, width), BF16)),
        *(pltpu.with_memory_space_constraint(a, pltpu.HBM) for a in (tile_place, tile_count, laplacian_blocks, features)),
        hbm=4,
        vmem=3 * lane_bytes + 3 * MIB,
        scratch=[
            pltpu.SMEM(tile_place.shape, jnp.int32),
            pltpu.SMEM(tile_count.shape, jnp.int32),
            pltpu.VMEM(laplacian_blocks.shape, BF16),
            pltpu.VMEM(features.shape, BF16),
            pltpu.SemaphoreType.DMA((4,)),
        ],
    )

    got = swap(features, "rep", 1)
    cut = lambda i: jnp.stack([own_cut[i], lax.dynamic_slice_in_dim(got, (rep ^ 2 * i) * width, width, 1)])
    pieces = [swap(cut(i), "rep", 2 * i) if i else cut(i) for i in range(chips)]
    own_rows, mate = after([jnp.stack(pieces), swap(dense, "rep", 1)])
    own_chip = [dense, mate]
    rows = [swap(own_rows, "blk", m) if m else own_rows for m in range(n_blk)]
    arrived = [swap(after([dense], pieces[i])[0], "rep", 2 * i) for i in range(1, chips)]
    lanes = [*own_chip]
    for got in arrived:
        lanes += [got, swap(got, "rep", 1)]

    strip_shape = jax.ShapeDtypeStruct((strip, width), BF16)
    vmem = n_rep * lane_bytes + 2 * rows_bytes + 4 * MIB
    macs = 2 * strip * n_blk * strip * width
    soon = [0, 1, *range(2, n_rep, 2)]
    late = [*range(3, n_rep, 2)]
    part = call(
        functools.partial(part_kernel, n_blk, tile, soon), jax.ShapeDtypeStruct((strip, width), F32),
        *[lanes[k] for k in soon], *rows,
        vmem=vmem, flops=1 << 35,
    )
    first = call(
        functools.partial(part_kernel, n_blk, tile, late), strip_shape,
        *[lanes[k] for k in late], *rows, part,
        vmem=vmem, flops=macs,
    )
    firsts = [swap(first, "blk", m) for m in range(1, n_blk)]
    others = [swap(lax.dynamic_slice_in_dim(first, (rep ^ k) * tile, tile, 0), "rep", k) for k in range(2, n_rep)]
    tied = after([*firsts, *others])
    firsts, others = [first, *tied[: n_blk - 1]], tied[n_blk - 1 :]
    seconds = call(
        functools.partial(second_kernel, n_blk, n_rep, tile),
        [jax.ShapeDtypeStruct((2 if k < 2 else 1, tile, width), BF16) for k in range(n_rep)],
        *lanes, *firsts, own_rows,
        vmem=vmem, flops=macs,
        scratch=[pltpu.VMEM((strip, width), F32)],
    )
    seconds = [swap(rows, "rep", k) if k else rows for k, rows in enumerate(seconds)]
    early = call(
        functools.partial(early_kernel, n_rep),
        jax.ShapeDtypeStruct((tile, feat), F32),
        features, order_weights, *others,
    )
    return call(
        functools.partial(last_kernel, n_rep),
        jax.ShapeDtypeStruct((tile, feat), BF16),
        early, order_weights, *seconds,
    )


def solution(mesh):
    in_specs = (
        P(("groups", "blk", "rep"), None),
        P(),
        P(("groups", "blk"), "rep", None, None, None, None),
        P(("groups", "blk"), "rep", None, None),
        P(("groups", "blk"), "rep", None),
    )
    out_specs = P(("groups", "blk", "rep"), None)
    return jax.shard_map(
        per_device, mesh=mesh, in_specs=in_specs, out_specs=out_specs, check_vma=False
    )
```

```python
import functools

import jax
import jax.numpy as jnp
from jax import lax
from jax.experimental import pallas as pl
from jax.experimental.pallas import tpu as pltpu
from jax.sharding import PartitionSpec as P

BF16 = jnp.bfloat16
F32 = jnp.float32
MIB = 1 << 20


def swap(array, axis, mask):
    peers = lax.axis_size(axis)
    return lax.ppermute(array, axis, [(i, i ^ mask) for i in range(peers)])


def near_by(array):
    if array.size * array.dtype.itemsize > MIB:
        return array
    return pltpu.with_memory_space_constraint(array, pltpu.VMEM)


def after(values, *earlier):
    left = pl.BlockSpec(memory_space=pl.ANY)
    return pl.pallas_call(
        lambda *refs: None,
        out_shape=[jax.ShapeDtypeStruct(v.shape, v.dtype) for v in values],
        in_specs=[left] * (len(values) + len(earlier)),
        out_specs=[left] * len(values),
        input_output_aliases={i: i for i in range(len(values))},
        compiler_params=pltpu.CompilerParams(vmem_limit_bytes=MIB),
    )(*values, *[near_by(e) for e in earlier])


def call(kernel, out_shapes, *args, scratch=(), vmem=4 * MIB, flops=0, hbm=0, earlier=()):
    whole = pl.BlockSpec(memory_space=pltpu.VMEM)
    left = pl.BlockSpec(memory_space=pl.ANY)
    home = pl.BlockSpec(memory_space=pltpu.HBM)
    size = sum(a.size * a.dtype.itemsize for a in args)
    n_args, n_all = len(args), len(args) + len(earlier)

    def body(*refs):
        kernel(*refs[:n_args], *refs[n_all:])

    return pl.pallas_call(
        body,
        out_shape=out_shapes,
        in_specs=[home] * hbm + [whole] * (n_args - hbm) + [left] * len(earlier),
        out_specs=jax.tree.map(lambda _: whole, out_shapes),
        scratch_shapes=list(scratch),
        compiler_params=pltpu.CompilerParams(vmem_limit_bytes=vmem),
        cost_estimate=pl.CostEstimate(flops=flops, bytes_accessed=size, transcendentals=0),
    )(*args[:hbm], *[near_by(a) for a in (*args[hbm:], *earlier)])


def dense_kernel(place_hbm, count_hbm, blocks_hbm, feats_hbm, dense_ref, cut_ref, *scratch):
    place_ref, count_ref, blocks_ref, feats_ref, sems = scratch
    n_blk, cap, tile = blocks_ref.shape[2:5]
    chips, width = cut_ref.shape[0], cut_ref.shape[2]
    pairs = [(blocks_hbm, blocks_ref), (place_hbm, place_ref), (count_hbm, count_ref), (feats_hbm, feats_ref)]
    copies = [pltpu.make_async_copy(a, b, sems.at[i]) for i, (a, b) in enumerate(pairs)]
    for copy in copies:
        copy.start()
    dense_ref[...] = jnp.zeros_like(dense_ref)
    own, rep = lax.axis_index("blk"), lax.axis_index("rep")
    for copy in copies:
        copy.wait()
    for i in range(chips):
        if width % 128 == 0:
            cut_ref[i] = feats_ref[:, pl.ds(pl.multiple_of((rep ^ 2 * i) * width, width), width)]
        else:
            for lane in range(feats_ref.shape[1] // width):

                @pl.when(lane == rep ^ 2 * i)
                def _():
                    cut_ref[i] = feats_ref[:, lane * width : (lane + 1) * width]

    for m in range(n_blk):
        j = own ^ m
        at = m * tile
        for slot in range(cap):

            @pl.when(slot < count_ref[0, 0, j])
            def _():
                row = pl.multiple_of(place_ref[0, 0, j, slot] * tile, tile)
                dense_ref[pl.ds(row, tile), at : at + tile] = blocks_ref[0, 0, j, slot]


def dot(a, b):
    return jnp.dot(a, b, preferred_element_type=F32)


def apply_lanes(lanes, n_blk, tile, rows_of):
    total = None
    for m in range(n_blk):
        columns = []
        for halves in lanes:
            each = n_blk // len(halves)
            at = (m % each) * tile
            columns.append(halves[m // each][:, at : at + tile])
        left = jnp.concatenate(columns, axis=1)
        right = jnp.concatenate([rows_of(m, k) for k in range(len(lanes))], axis=0)
        part = dot(left, right)
        total = part if total is None else total + part
    return total


def grouped(refs, sizes):
    lists, refs = [], list(refs)
    for size in sizes:
        lists.append(refs[:size])
        refs = refs[size:]
    return lists, refs


def part_kernel(n_blk, tile, masks, sizes, *refs):
    lanes, refs = grouped(refs, sizes)
    pieces, more, out_ref = refs[:n_blk], refs[n_blk:-1], refs[-1]
    total = apply_lanes(lanes, n_blk, tile, lambda m, i: pieces[m][masks[i] // 2, masks[i] % 2])
    if more:
        total = total + more[0][...]
    out_ref[...] = total.astype(out_ref.dtype)


def second_kernel(n_blk, n_rep, tile, sizes, *refs):
    lanes, refs = grouped(refs, sizes)
    firsts, feats, outs, total_ref = refs[:n_blk], refs[n_blk], refs[n_blk + 1 : -1], refs[-1]
    rep = lax.axis_index("rep")
    rows = [pl.ds(pl.multiple_of((rep ^ k) * tile, tile), tile) for k in range(n_rep)]
    total_ref[...] = apply_lanes(lanes, n_blk, tile, lambda m, k: firsts[m][rows[k], :])
    for k, out_ref in enumerate(outs):
        if k < 2:
            out_ref[1] = firsts[0][rows[k], :]
        out_ref[0] = (2.0 * total_ref[rows[k], :] - feats[k // 2, k % 2].astype(F32)).astype(BF16)


def weigh(pieces, weight_ref, order, masks):
    rep, width = lax.axis_index("rep"), pieces[0].shape[1]
    rows = [pl.ds(pl.multiple_of((rep ^ k) * width, width), width) for k in masks]
    weights = [weight_ref[order, r, :] for r in rows]
    return dot(jnp.concatenate(pieces, axis=1), jnp.concatenate(weights, axis=0))


def early_kernel(n_rep, feats_ref, weight_ref, *refs):
    others, out_ref = [ref[...] for ref in refs[:-1]], refs[-1]
    out_ref[...] = dot(feats_ref[...], weight_ref[0]) + weigh(others, weight_ref, 1, range(2, n_rep))


def last_kernel(n_rep, early_ref, weight_ref, *refs):
    pieces, out_ref = refs[:-1], refs[-1]
    total = early_ref[...] + weigh([piece[1] for piece in pieces[:2]], weight_ref, 1, range(2))
    total = total + weigh([piece[0] for piece in pieces], weight_ref, 2, range(n_rep))
    out_ref[...] = total.astype(BF16)


def per_device(features, order_weights, laplacian_blocks, tile_place, tile_count):
    n_blk, n_rep = lax.axis_size("blk"), lax.axis_size("rep")
    rep = lax.axis_index("rep")
    chips = n_rep // 2
    tile, feat = features.shape
    strip = n_rep * tile
    width = feat // n_rep
    lane_bytes = 2 * strip * n_blk * tile
    rows_bytes = 2 * strip * n_blk * max(width, 128)

    dense, own_cut = call(
        dense_kernel,
        (jax.ShapeDtypeStruct((strip, n_blk * tile), BF16), jax.ShapeDtypeStruct((chips, tile, width), BF16)),
        *(pltpu.with_memory_space_constraint(a, pltpu.HBM) for a in (tile_place, tile_count, laplacian_blocks, features)),
        hbm=4,
        vmem=3 * lane_bytes + 3 * MIB,
        scratch=[
            pltpu.SMEM(tile_place.shape, jnp.int32),
            pltpu.SMEM(tile_count.shape, jnp.int32),
            pltpu.VMEM(laplacian_blocks.shape, BF16),
            pltpu.VMEM(features.shape, BF16),
            pltpu.SemaphoreType.DMA((4,)),
        ],
    )

    got = swap(features, "rep", 1)
    cut = lambda i: jnp.stack([own_cut[i], lax.dynamic_slice_in_dim(got, (rep ^ 2 * i) * width, width, 1)])
    pieces = [swap(cut(i), "rep", 2 * i) if i else cut(i) for i in range(chips)]
    own_rows, mate = after([jnp.stack(pieces), swap(dense, "rep", 1)])
    own_chip = [dense, mate]
    rows = [swap(own_rows, "blk", m) if m else own_rows for m in range(n_blk)]
    lanes = [[lane] for lane in own_chip]
    middle = n_blk // 2 * tile
    for i in range(1, chips):
        parts = after([p for p in (dense[:, :middle], dense[:, middle:])], pieces[i])
        arrived = [swap(part, "rep", 2 * i) for part in parts]
        lanes += [arrived, [swap(got, "rep", 1) for got in arrived]]

    strip_shape = jax.ShapeDtypeStruct((strip, width), BF16)
    vmem = n_rep * lane_bytes + 2 * rows_bytes + 4 * MIB
    macs = 2 * strip * n_blk * strip * width
    soon = [0, 1, *range(2, n_rep, 2)]
    late = [*range(3, n_rep, 2)]
    part = call(
        functools.partial(part_kernel, n_blk, tile, soon, [len(lanes[k]) for k in soon]), jax.ShapeDtypeStruct((strip, width), F32),
        *[h for k in soon for h in lanes[k]], *rows,
        vmem=vmem, flops=1 << 35,
    )
    first = call(
        functools.partial(part_kernel, n_blk, tile, late, [len(lanes[k]) for k in late]), strip_shape,
        *[h for k in late for h in lanes[k]], *rows, part,
        vmem=vmem, flops=macs,
    )
    firsts = [swap(first, "blk", m) for m in range(1, n_blk)]
    others = [swap(lax.dynamic_slice_in_dim(first, (rep ^ k) * tile, tile, 0), "rep", k) for k in range(2, n_rep)]
    tied = after([*firsts, *others])
    firsts, others = [first, *tied[: n_blk - 1]], tied[n_blk - 1 :]
    seconds = call(
        functools.partial(second_kernel, n_blk, n_rep, tile, [len(lane) for lane in lanes]),
        [jax.ShapeDtypeStruct((2 if k < 2 else 1, tile, width), BF16) for k in range(n_rep)],
        *[h for lane in lanes for h in lane], *firsts, own_rows,
        vmem=vmem, flops=macs,
        scratch=[pltpu.VMEM((strip, width), F32)],
    )
    seconds = [swap(rows, "rep", k) if k else rows for k, rows in enumerate(seconds)]
    early = call(
        functools.partial(early_kernel, n_rep),
        jax.ShapeDtypeStruct((tile, feat), F32),
        features, order_weights, *others,
    )
    return call(
        functools.partial(last_kernel, n_rep),
        jax.ShapeDtypeStruct((tile, feat), BF16),
        early, order_weights, *seconds,
    )


def solution(mesh):
    in_specs = (
        P(("groups", "blk", "rep"), None),
        P(),
        P(("groups", "blk"), "rep", None, None, None, None),
        P(("groups", "blk"), "rep", None, None),
        P(("groups", "blk"), "rep", None),
    )
    out_specs = P(("groups", "blk", "rep"), None)
    return jax.shard_map(
        per_device, mesh=mesh, in_specs=in_specs, out_specs=out_specs, check_vma=False
    )
```
